256 devices in a mesh: cp: 32 (over z, x_lo, core), tp: 8 (over y, x_hi).
Axes of the slice: x: 4 (x_hi: 2, x_lo: 2; x = x_hi * 2 + x_lo), y: 4, z: 8, core: 2. Of those that a mesh axis runs over, the one named last changes fastest.
Arguments:
- queries: bfloat16 [16384, 8192], P('cp', 'tp'), may hold values from -128 to 128
- keys: bfloat16 [16384, 1024], P(('cp', 'tp')), may hold values from -6 to 6
- values: bfloat16 [16384, 1024], P(('cp', 'tp')), may hold values from -6 to 6
- doc_ids: int32 [16384], P('cp'), may hold values from 0 to 31, never falling along the last dimension, each value on 1 to 4096 neighbouring positions
Outputs:
- attended: bfloat16 [16384, 8192], P('cp', 'tp')
The draws below stay inside these ranges and needn't reach their ends.
Inputs may be any that keep to these rules, and one draw needn't show every extreme that they name: `doc_ids`: never falls along the positions; every document has 1 to 4096 positions and one has exactly 4096; every number from 0 to 31 is used.
All inputs are finite; a program needn't handle non-finite values.
Results may differ from the reference program's by a relative error of at most 0.0035.
Values may be sent and summed in bfloat16 or wider, within the bound.
No kernel may reach another device: no remote copies, remote signals or barrier semaphores. Data moves between devices by JAX's collectives and lax.ppermute only.
A program may use at most 64 MiB of HBM per device.

```python
import math
import jax
import jax.numpy as jnp
import numpy as np
from jax import lax

QUERY_HEADS = 64
KEY_VALUE_HEADS = 8
HEAD_WIDTH = 128
BLOCK_TOKENS = 512
PACKED_TOKENS = 16384
DOC_MOST = 4096
DOCS = 32
HOPS = 8
N_CP = 32


def shared_keys(key):
    return jnp.clip(jax.random.normal(key, (PACKED_TOKENS, KEY_VALUE_HEADS * HEAD_WIDTH), jnp.float32), -6.0, 6.0)


def draw_keys(key, part):
    base_offset = shared_keys(key)
    return base_offset.astype(jnp.bfloat16)


def draw_queries(key, part):
    key = jax.random.fold_in(key, 5)
    first = jax.random.fold_in(key, 0)
    result = jax.random.normal(first, (PACKED_TOKENS, QUERY_HEADS * HEAD_WIDTH), jnp.float32)
    return jnp.clip(result, -128.0, 128.0).astype(jnp.bfloat16)


def levels(rng, extent, cuts, smallest, largest):
    def one(axis_at, shards_of):
        heights = jax.random.uniform(jax.random.fold_in(jax.random.fold_in(rng, 6), axis_at), (shards_of,), jnp.float32, smallest / len(cuts), largest / len(cuts))
        return jnp.repeat(jnp.exp(heights), extent[axis_at] // shards_of).reshape((-1,) + (1,) * (len(extent) - axis_at - 1))

    gain = one(*cuts[0])
    for cut in cuts[1:]:
        gain = gain * one(*cut)
    return gain


def profile(amount, total, most, lean):
    portions = [(1 << 20) // math.isqrt(standing ** lean) + 1 for standing in range(2, amount + 1)]
    spare, given = total - most - (amount - 1), [1] * (amount - 1)
    while spare > 0:
        movable = [i for i in range(amount - 1) if given[i] < most]
        pool, left = sum([portions[i] for i in movable]), spare
        for i in movable:
            more = min(most - given[i], max(1, left * portions[i] // pool), spare)
            given[i] = given[i] + more
            spare = spare - more
    return np.array([most] + given)


def ragged(key, amount, total, reach, slope):
    if amount == 2:
        one = jax.random.randint(key, (), max(1, total - reach), min(reach, total - 1) + 1)
        return jnp.stack([one, total - one])
    sizes = jnp.asarray(profile(amount, total, reach, slope), jnp.int32)
    pairs = (amount - 1) // 2
    giver, sink = sizes[1:1 + 2 * pairs:2], sizes[2:2 + 2 * pairs:2]
    slack = jnp.minimum(giver - 1, reach - sink)
    shifted = jax.random.randint(jax.random.fold_in(key, 1), (pairs,), 0, 1 << 20) % (slack + 1)
    sizes = sizes.at[1:1 + 2 * pairs:2].set(giver - shifted).at[2:2 + 2 * pairs:2].set(sink + shifted)
    return sizes[jax.random.permutation(jax.random.fold_in(key, 2), amount)]


def normal_values(stream_key, dims, spread, reach, shards=(), kind=jnp.bfloat16):
    values = spread * jax.random.normal(stream_key, dims, jnp.float32)
    if shards:
        values = values * levels(stream_key, dims, shards, -0.22, 0.18)
    return jnp.clip(values, -reach, reach).astype(kind)


def setup_inputs(seed: int = 0) -> dict:
    key_list = jax.random.split(jax.random.key(seed), 5)
    return {
        "queries": draw_queries(jax.random.fold_in(key_list[4], 71), 0),
        "keys": draw_keys(jax.random.fold_in(key_list[4], 71), 0),
        "values": normal_values(key_list[2], (PACKED_TOKENS, KEY_VALUE_HEADS * HEAD_WIDTH), 1.0, 6.0, ((0, 256),)),
        "doc_ids": jnp.searchsorted(jnp.cumsum(ragged(key_list[3], DOCS, PACKED_TOKENS, DOC_MOST, 2)), jnp.arange(PACKED_TOKENS), side="right").astype(jnp.int32),
    }


def block_terms(query_block, key_block, value_block, allowed):
    scores = jnp.einsum("qhgd,khd->hgqk", query_block.astype(jnp.float32), key_block.astype(jnp.float32)) * (HEAD_WIDTH ** -0.5)
    masked = jnp.where(allowed, scores, -1e30)
    block_max = jnp.max(masked, axis=-1)
    weights = jnp.where(allowed, jnp.exp(masked - block_max[..., None]), 0.0)
    block_total = jnp.sum(weights, axis=-1)
    rounded = lax.optimization_barrier(weights.astype(jnp.bfloat16))
    block_out = jnp.einsum("hgqk,khd->qhgd", rounded.astype(jnp.float32), value_block.astype(jnp.float32))
    return block_max, block_out, block_total


def merge_state(running_state, terms):
    old_max, old_out, old_total = running_state
    new_max, new_out, new_total = terms
    joint = jnp.maximum(old_max, new_max)
    keep = jnp.exp(old_max - joint)
    take = jnp.exp(new_max - joint)
    out = old_out * jnp.transpose(keep, (2, 0, 1))[..., None] + new_out * jnp.transpose(take, (2, 0, 1))[..., None]
    return joint, out, old_total * keep + new_total * take


def reference(queries, keys, values, doc_ids):
    query_groups = QUERY_HEADS // KEY_VALUE_HEADS
    query_everything = queries.reshape(N_CP, BLOCK_TOKENS, KEY_VALUE_HEADS, query_groups, HEAD_WIDTH)
    key_everything = keys.reshape(PACKED_TOKENS, KEY_VALUE_HEADS, HEAD_WIDTH)
    value_everything = values.reshape(PACKED_TOKENS, KEY_VALUE_HEADS, HEAD_WIDTH)
    offsets = jnp.arange(BLOCK_TOKENS, dtype=jnp.int32)

    def one_block(index):
        query_block = query_everything[index]
        query_pos = index * BLOCK_TOKENS + offsets
        query_doc = lax.dynamic_slice_in_dim(doc_ids, (index * BLOCK_TOKENS).astype(jnp.int32), BLOCK_TOKENS)
        running_state = (jnp.full((KEY_VALUE_HEADS, query_groups, BLOCK_TOKENS), -1e30, jnp.float32),
                 jnp.zeros((BLOCK_TOKENS, KEY_VALUE_HEADS, query_groups, HEAD_WIDTH), jnp.float32),
                 jnp.zeros((KEY_VALUE_HEADS, query_groups, BLOCK_TOKENS), jnp.float32))
        for back in range(HOPS + 1):
            source = index - back
            start = (jnp.maximum(source, 0) * BLOCK_TOKENS).astype(jnp.int32)
            key_pos = source * BLOCK_TOKENS + offsets
            key_doc = lax.dynamic_slice_in_dim(doc_ids, start, BLOCK_TOKENS)
            allowed = (query_doc[:, None] == key_doc[None, :]) & (key_pos[None, :] <= query_pos[:, None]) & (key_pos[None, :] >= 0)
            key_block = lax.dynamic_slice_in_dim(key_everything, start, BLOCK_TOKENS)
            value_block = lax.dynamic_slice_in_dim(value_everything, start, BLOCK_TOKENS)
            running_state = lax.cond(jnp.any(allowed),
                             lambda s: merge_state(s, block_terms(query_block, key_block, value_block, allowed)),
                             lambda s: s, running_state)
        final = running_state[1] / jnp.transpose(running_state[2], (2, 0, 1))[..., None]
        return final.astype(jnp.bfloat16)

    result = lax.map(one_block, jnp.arange(N_CP, dtype=jnp.int32))
    return result.reshape(PACKED_TOKENS, QUERY_HEADS * HEAD_WIDTH)
```

```python
import functools

import jax
import jax.numpy as jnp
from jax import lax
from jax.experimental import pallas as pl
from jax.experimental.pallas import tpu as pltpu
from jax.sharding import PartitionSpec as P

HEADS = 8
TP = 8
WIDTH = 128
BLOCK = 512
CHUNK = BLOCK // TP
TILE = 128
TILES = BLOCK // TILE
COLS = HEADS * TILE
ALL = TILES * COLS
AUG = WIDTH + 16
PACK = BLOCK + 4 * AUG
SCALE = WIDTH**-0.5 * 1.4426950408889634
NEVER = -1e30
LIMIT = 2.0**100
f32, bf16 = jnp.float32, jnp.bfloat16
VMEM = pl.BlockSpec(memory_space=pltpu.VMEM)


def dot(a, b):
    return jnp.dot(a, b, preferred_element_type=f32)


def call(kernel, outs, operands, scratch=(), flops=0, vmem=32):
    return pl.pallas_call(
        kernel,
        out_shape=outs,
        in_specs=[VMEM] * len(operands),
        out_specs=jax.tree.map(lambda _: VMEM, outs),
        scratch_shapes=list(scratch),
        compiler_params=pltpu.CompilerParams(vmem_limit_bytes=vmem << 20),
        cost_estimate=pl.CostEstimate(flops=flops, bytes_accessed=4 << 20, transcendentals=0),
    )(*operands)


def split_heads(k_ref, v_ref, out_ref):
    for h in range(TP):
        cols = slice(h * WIDTH, (h + 1) * WIDTH)
        out_ref[h, :CHUNK] = k_ref[:, cols]
        out_ref[h, CHUNK:] = v_ref[:, cols]


def pack_block(kv_ref, docs_ref, out_ref):
    for t in range(TP):
        out_ref[t * CHUNK : (t + 1) * CHUNK] = kv_ref[t, :CHUNK]
    for c in range(4):
        at = BLOCK + c * AUG
        v = jnp.concatenate([kv_ref[2 * c, CHUNK:], kv_ref[2 * c + 1, CHUNK:]], axis=0)
        out_ref[at : at + WIDTH] = v.T
        row = docs_ref[:, c * TILE : (c + 1) * TILE]
        out_ref[at + WIDTH : at + AUG] = jnp.broadcast_to(row, (16, TILE)).astype(bf16)


def tiled(row):
    return jnp.concatenate([row] * HEADS, axis=1)


def own_mask(first, keys):
    u, t = keys
    return (u <= t) & (u >= first)


def own_part(q_ref, own_ref, docs_ref, start_ref, qt_ref, bias_ref, acc_ref, vt_ref):
    ones = jnp.ones((16, TILE), bf16)
    for c in range(4):
        at = BLOCK + c * AUG
        vt_ref[:WIDTH, c * TILE : (c + 1) * TILE] = own_ref[at : at + WIDTH]
        vt_ref[WIDTH:, c * TILE : (c + 1) * TILE] = ones
    first_doc = docs_ref[:, :1]
    for i in range(TILES):
        here = slice(i * TILE, (i + 1) * TILE)
        qt = jnp.concatenate(
            [q_ref[here, h * WIDTH : (h + 1) * WIDTH].T for h in range(HEADS)], axis=1
        )
        cols = slice(i * COLS, (i + 1) * COLS)
        qt_ref[:, cols] = qt
        count = (i + 1) * TILE
        u = lax.broadcasted_iota(jnp.int32, (count, TILE), 0)
        t = lax.broadcasted_iota(jnp.int32, (count, TILE), 1) + i * TILE
        allowed = own_mask(start_ref[:, here], (u, t))
        allowed = jnp.concatenate([allowed] * HEADS, axis=1)
        scores = jnp.where(allowed, dot(own_ref[:count], qt), NEVER)
        bias = jnp.max(scores, axis=0, keepdims=True) * SCALE
        weights = jnp.exp2(scores * SCALE - bias).astype(bf16)
        acc_ref[:, cols] = dot(vt_ref[:, :count], weights)
        joins = tiled(jnp.broadcast_to(first_doc, (1, TILE)) == docs_ref[:, here])
        bias_ref[0:1, cols] = bias
        bias_ref[1:2, cols] = jnp.where(joins, bias, -NEVER)
        bias_ref[2:8, cols] = jnp.zeros((6, COLS), f32)


def gather_block(block_ref, at, doc, k_ref, vt_ref):
    k_ref[pl.ds(at, BLOCK), :] = block_ref[:BLOCK]
    count = jnp.zeros((1, TILE), f32)
    for c in range(4):
        rows = BLOCK + c * AUG
        mask = block_ref[rows + WIDTH : rows + AUG] == doc
        lanes = pl.ds(at + c * TILE, TILE)
        mask1 = mask[:1]
        vt_ref[:WIDTH, lanes] = jnp.where(
            jnp.broadcast_to(mask1, (WIDTH, TILE)), block_ref[rows : rows + WIDTH], jnp.zeros((), bf16)
        )
        vt_ref[WIDTH:, lanes] = jnp.where(mask, jnp.ones((), bf16), jnp.zeros((), bf16))
        count = count + mask1.astype(f32)
    return count


def add_keys(blocks, tiles, qt_ref, bias_ref, k_ref, vt_ref, acc_in, acc_out):
    def tile(i, _):
        cols = pl.ds(pl.multiple_of(i * COLS, COLS), COLS)
        qt, bias = qt_ref[:, cols], bias_ref[1:2, cols]
        weights = jnp.exp2(dot(k_ref[: blocks * BLOCK], qt) * SCALE - bias).astype(bf16)
        acc_out[:, cols] = acc_in[:, cols] + dot(vt_ref[:, : blocks * BLOCK], weights)
        return 0

    lax.fori_loop(0, tiles, tile, 0)


def parity_places(core, base):
    mine = pl.multiple_of(base + (1 - core) * BLOCK, BLOCK)
    other = pl.multiple_of(base + core * BLOCK, BLOCK)
    return mine, other


def first_and_reach(docs_ref):
    docs = docs_ref[...]
    doc = docs[:, :1]
    rows = jnp.sum((docs == doc).astype(f32)).astype(jnp.int32)
    return doc.astype(bf16), (rows + TILE - 1) // TILE


def blocks_needed(count):
    keys = jnp.sum(count).astype(jnp.int32)
    return (keys + BLOCK - 1) // BLOCK


def near_part(core_ref, docs_ref, qt_ref, bias_ref, acc_in, pair_ref, a2, b2, a4, b4, acc_out, k_ref, vt_ref):
    core = core_ref[0]
    doc, tiles = first_and_reach(docs_ref)
    pair_doc = jnp.where(core == 1, doc, -jnp.ones_like(doc))
    count = gather_block(pair_ref, 0, pair_doc, k_ref, vt_ref)
    base = pl.multiple_of(core * BLOCK, BLOCK)
    for own, other in ((a2, b2), (a4, b4)):
        x, y = parity_places(core, base)
        count += gather_block(own, x, doc, k_ref, vt_ref)
        count += gather_block(other, y, doc, k_ref, vt_ref)
        base = pl.multiple_of(base + 2 * BLOCK, BLOCK)
    need = blocks_needed(count)
    acc_out[...] = acc_in[...]
    for blocks in range(1, 6):

        @pl.when(need == blocks)
        def _(blocks=blocks):
            add_keys(blocks, tiles, qt_ref, bias_ref, k_ref, vt_ref, acc_out, acc_out)


def far_part(
    core_ref, docs_ref, start_ref, qt_ref, bias_ref, acc_in, own_ref, pair_ref, a2, b2, a4, b4, a6, b6, a8, b8,
    out_ref, k_ref, vt_ref, acc_ref, flag_ref,
):
    core = core_ref[0]
    doc, tiles = first_and_reach(docs_ref)
    base = 0
    count = jnp.zeros((1, TILE), f32)
    for own, other in ((a6, b6), (a8, b8)):
        x, y = parity_places(core, base)
        count += gather_block(own, x, doc, k_ref, vt_ref)
        count += gather_block(other, y, doc, k_ref, vt_ref)
        base += 2 * BLOCK
    need = blocks_needed(count)
    acc_ref[...] = acc_in[...]
    for blocks in range(1, 5):

        @pl.when(need == blocks)
        def _(blocks=blocks):
            add_keys(blocks, tiles, qt_ref, bias_ref, k_ref, vt_ref, acc_ref, acc_ref)

    total = acc_ref[WIDTH : WIDTH + 1]
    fine = jnp.min((total < LIMIT).astype(f32))

    @pl.when(fine < 0.5)
    def _():
        pair_doc = jnp.where(core == 1, doc, -jnp.ones_like(doc))
        blocks = ((pair_ref, pair_doc), (a2, doc), (b2, doc), (a4, doc), (b4, doc), (a6, doc), (b6, doc), (a8, doc), (b8, doc))
        for i in range(TILES):
            cols = slice(i * COLS, (i + 1) * COLS)
            flag_ref[0:1, cols] = bias_ref[0:1, cols]
        first = first_acc(own_ref, start_ref, qt_ref, bias_ref, vt_ref)
        for i in range(TILES):
            acc_ref[:, i * COLS : (i + 1) * COLS] = first(i)
        for block_ref, block_doc in blocks:
            gather_block(block_ref, 0, block_doc, k_ref, vt_ref)
            mask = vt_ref[WIDTH : WIDTH + 1, :BLOCK].astype(f32)
            mask = jnp.concatenate(
                [jnp.broadcast_to(mask[:, c * TILE : (c + 1) * TILE], (TILE, TILE)).T for c in range(4)], axis=0
            )

            def tile(i, _, mask=mask):
                cols = pl.ds(pl.multiple_of(i * COLS, COLS), COLS)
                joins = bias_ref[1:2, cols] < 1e29
                allowed = (jnp.concatenate([mask] * HEADS, axis=1) > 0.5) & joins
                scores = jnp.where(allowed, dot(k_ref[:BLOCK], qt_ref[:, cols]), NEVER)
                old = flag_ref[0:1, cols]
                new = jnp.maximum(old, jnp.max(scores, axis=0, keepdims=True) * SCALE)
                weights = jnp.exp2(scores * SCALE - new).astype(bf16)
                acc_ref[:, cols] = acc_ref[:, cols] * jnp.exp2(old - new) + dot(vt_ref[:, :BLOCK], weights)
                flag_ref[0:1, cols] = new
                return 0

            lax.fori_loop(0, TILES, tile, 0)

    def finish(i, _):
        cols = pl.ds(pl.multiple_of(i * COLS, COLS), COLS)
        final = (acc_ref[:WIDTH, cols] / acc_ref[WIDTH : WIDTH + 1, cols]).astype(bf16)
        rows = pl.ds(pl.multiple_of(i * TILE, TILE), TILE)
        for h in range(HEADS):
            out_ref[rows, h * WIDTH : (h + 1) * WIDTH] = final[:, h * TILE : (h + 1) * TILE].T
        return 0

    lax.fori_loop(0, TILES, finish, 0)


def first_acc(own_ref, start_ref, qt_ref, bias_ref, vt_ref):
    for c in range(4):
        at = BLOCK + c * AUG
        vt_ref[:WIDTH, c * TILE : (c + 1) * TILE] = own_ref[at : at + WIDTH]
        vt_ref[WIDTH:, c * TILE : (c + 1) * TILE] = jnp.ones((16, TILE), bf16)

    def tile(i):
        cols = slice(i * COLS, (i + 1) * COLS)
        count = (i + 1) * TILE
        u = lax.broadcasted_iota(jnp.int32, (count, TILE), 0)
        t = lax.broadcasted_iota(jnp.int32, (count, TILE), 1) + i * TILE
        allowed = own_mask(start_ref[:, i * TILE : (i + 1) * TILE], (u, t))
        allowed = jnp.concatenate([allowed] * HEADS, axis=1)
        scores = jnp.where(allowed, dot(own_ref[:count], qt_ref[:, cols]), NEVER)
        weights = jnp.exp2(scores * SCALE - bias_ref[0:1, cols]).astype(bf16)
        return dot(vt_ref[:, :count], weights)

    return tile


def back(value, steps):
    count = lax.axis_size("cp")
    return lax.ppermute(value, "cp", [(s, s + steps) for s in range(count - steps)])


def other_core(value):
    return lax.ppermute(value, "cp", [(s, s ^ 1) for s in range(lax.axis_size("cp"))])


def per_device(queries, keys, values, doc_ids):
    shape = jax.ShapeDtypeStruct
    core = (lax.axis_index("cp") % 2).astype(jnp.int32).reshape(1)
    docs = (doc_ids + 1).astype(f32).reshape(1, BLOCK)
    start = jnp.sum(doc_ids[None, :] < doc_ids[:, None], axis=1).astype(jnp.int32).reshape(1, BLOCK)

    split = call(split_heads, shape((TP, 2 * CHUNK, WIDTH), bf16), (keys, values))
    mine = lax.all_to_all(split, "tp", split_axis=0, concat_axis=0, tiled=True)
    own = call(pack_block, shape((PACK, WIDTH), bf16), (mine, docs))

    a4 = back(own, 4)
    a2 = back(own, 2)
    pair = other_core(own)
    state = (shape((WIDTH, ALL), bf16), shape((8, ALL), f32), shape((AUG, ALL), f32))
    qt, bias, acc = call(
        own_part, state, (queries, own, docs, start), [pltpu.VMEM((AUG, BLOCK), bf16)], flops=2 * 10**9
    )
    a8 = back(a4, 4)
    a6 = back(a4, 2)
    b2, b4 = other_core(jnp.stack([a2, a4]))
    acc = near(core, docs, qt, bias, acc, pair, a2, b2, a4, b4)
    b6, b8 = other_core(jnp.stack([a6, a8]))
    return far(core, docs, start, qt, bias, acc, own, pair, a2, b2, a4, b4, a6, b6, a8, b8)


def near(core, *operands):
    return pl.pallas_call(
        near_part,
        out_shape=jax.ShapeDtypeStruct((AUG, ALL), f32),
        in_specs=[pl.BlockSpec(memory_space=pltpu.SMEM)] + [VMEM] * len(operands),
        out_specs=VMEM,
        scratch_shapes=[pltpu.VMEM((6 * BLOCK, WIDTH), bf16), pltpu.VMEM((AUG, 6 * BLOCK), bf16)],
        compiler_params=pltpu.CompilerParams(vmem_limit_bytes=40 << 20),
        cost_estimate=pl.CostEstimate(flops=8 * 10**9, bytes_accessed=6 << 20, transcendentals=0),
    )(core, *operands)


def far(core, *operands):
    return pl.pallas_call(
        far_part,
        out_shape=jax.ShapeDtypeStruct((BLOCK, HEADS * WIDTH), bf16),
        in_specs=[pl.BlockSpec(memory_space=pltpu.SMEM)] + [VMEM] * len(operands),
        out_specs=VMEM,
        scratch_shapes=[
            pltpu.VMEM((4 * BLOCK, WIDTH), bf16),
            pltpu.VMEM((AUG, 4 * BLOCK), bf16),
            pltpu.VMEM((AUG, ALL), f32),
            pltpu.VMEM((8, ALL), f32),
        ],
        compiler_params=pltpu.CompilerParams(vmem_limit_bytes=40 << 20),
        cost_estimate=pl.CostEstimate(flops=8 * 10**9, bytes_accessed=6 << 20, transcendentals=0),
    )(core, *operands)


def solution(mesh):
    placed = (P("cp", "tp"), P(("cp", "tp"), None), P(("cp", "tp"), None), P("cp"))
    return jax.shard_map(per_device, mesh=mesh, in_specs=placed, out_specs=P("cp", "tp"), check_vma=False)
```

```python
import functools

import jax
import jax.numpy as jnp
from jax import lax
from jax.experimental import pallas as pl
from jax.experimental.pallas import tpu as pltpu
from jax.sharding import PartitionSpec as P

HEADS = 8
TP = 8
WIDTH = 128
BLOCK = 512
CHUNK = BLOCK // TP
TILE = 128
TILES = BLOCK // TILE
COLS = HEADS * TILE
ALL = TILES * COLS
AUG = WIDTH + 16
PACK = BLOCK + 4 * AUG
SCALE = WIDTH**-0.5 * 1.4426950408889634
NEVER = -1e30
LIMIT = 2.0**100
f32, bf16 = jnp.float32, jnp.bfloat16
SPLIT_VMEM = 60
OWN_COST = (10**11, 1 << 20)
NEAR_COST = (10**4, 10**4)
NEXT_COST = (10**4, 10**4)
FAR_AFTER = 0
NEAR_AFTER = 0
VMEM = pl.BlockSpec(memory_space=pltpu.VMEM)
SMEM = pl.BlockSpec(memory_space=pltpu.SMEM)
ANY = pl.BlockSpec(memory_space=pl.ANY)
HBM = pl.BlockSpec(memory_space=pltpu.HBM)


def dot(a, b):
    return jnp.dot(a, b, preferred_element_type=f32)


def call(kernel, outs, operands, scratch=(), cost=(10**4, 10**4), vmem=32, specs=None, out_specs=None):
    return pl.pallas_call(
        kernel,
        out_shape=outs,
        in_specs=specs or [VMEM] * len(operands),
        out_specs=out_specs or jax.tree.map(lambda _: VMEM, outs),
        scratch_shapes=list(scratch),
        compiler_params=pltpu.CompilerParams(vmem_limit_bytes=vmem << 20),
        cost_estimate=pl.CostEstimate(flops=cost[0], bytes_accessed=cost[1], transcendentals=0),
    )(*operands)


def split_heads(k_hbm, v_hbm, out_ref, kv_ref, sems):
    copies = [pltpu.make_async_copy(ref, kv_ref.at[j], sems.at[j]) for j, ref in enumerate((k_hbm, v_hbm))]
    for copy in copies:
        copy.start()
    for copy in copies:
        copy.wait()
    for h in range(TP):
        for j in range(2):
            out_ref[h, j * CHUNK : (j + 1) * CHUNK] = kv_ref[j, :, h * WIDTH : (h + 1) * WIDTH]


def transpose_queries(q_hbm, qt_ref, q_ref, sem):
    copy = pltpu.make_async_copy(q_hbm, q_ref, sem)
    copy.start()
    copy.wait()
    for i in range(TILES):
        for h in range(HEADS):
            at = i * COLS + h * TILE
            qt_ref[:, at : at + TILE] = q_ref[i * TILE : (i + 1) * TILE, h * WIDTH : (h + 1) * WIDTH].T


def stack(count, *refs):
    out_ref = refs[-1]
    for j, block in enumerate(refs[:count]):
        out_ref[j] = block[...]


def pack_block(kv_ref, docs_ref, dep0_ref, dep1_ref, out_ref):
    del dep0_ref, dep1_ref
    for t in range(TP):
        out_ref[t * CHUNK : (t + 1) * CHUNK] = kv_ref[t, :CHUNK]
    for c in range(4):
        at = BLOCK + c * AUG
        v = jnp.concatenate([kv_ref[2 * c, CHUNK:], kv_ref[2 * c + 1, CHUNK:]], axis=0)
        out_ref[at : at + WIDTH] = v.T
        row = docs_ref[:, c * TILE : (c + 1) * TILE]
        out_ref[at + WIDTH : at + AUG] = jnp.broadcast_to(row, (16, TILE)).astype(bf16)


def tiled(row):
    return jnp.concatenate([row] * HEADS, axis=1)


def own_mask(start_ref, i):
    count = (i + 1) * TILE
    u = lax.broadcasted_iota(jnp.int32, (count, TILE), 0)
    t = lax.broadcasted_iota(jnp.int32, (count, TILE), 1) + i * TILE
    allowed = (u <= t) & (u >= start_ref[:, i * TILE : (i + 1) * TILE])
    return jnp.concatenate([jnp.where(allowed, 0.0, NEVER)] * HEADS, axis=1)


def own_part(qt_ref, own_ref, docs_ref, start_ref, bias_ref, acc_ref, vt_ref):
    ones = jnp.ones((16, TILE), bf16)
    for c in range(4):
        at = BLOCK + c * AUG
        vt_ref[:WIDTH, c * TILE : (c + 1) * TILE] = own_ref[at : at + WIDTH]
        vt_ref[WIDTH:, c * TILE : (c + 1) * TILE] = ones
    first_doc = docs_ref[:, :1]
    for i in range(TILES):
        here = slice(i * TILE, (i + 1) * TILE)
        cols = slice(i * COLS, (i + 1) * COLS)
        count = (i + 1) * TILE
        scores = dot(own_ref[:count], qt_ref[:, cols]) * SCALE + own_mask(start_ref, i)
        bias = jnp.max(scores, axis=0, keepdims=True)
        weights = jnp.exp2(scores - bias).astype(bf16)
        acc_ref[:, cols] = dot(vt_ref[:, :count], weights)
        joins = tiled(jnp.broadcast_to(first_doc, (1, TILE)) == docs_ref[:, here])
        bias_ref[0:1, cols] = bias
        bias_ref[1:2, cols] = jnp.where(joins, bias, -NEVER)
        bias_ref[2:8, cols] = jnp.zeros((6, COLS), f32)


def gather_block(block_ref, at, doc, k_ref, vt_ref):
    count = jnp.zeros((1, TILE), f32)
    for c in range(4):
        rows = BLOCK + c * AUG
        mask = block_ref[rows + WIDTH : rows + AUG] == doc
        lanes = pl.ds(at + (3 - c) * TILE, TILE)
        k_ref[lanes, :] = block_ref[c * TILE : (c + 1) * TILE]
        mask1 = mask[:1]
        vt_ref[:WIDTH, lanes] = jnp.where(
            jnp.broadcast_to(mask1, (WIDTH, TILE)), block_ref[rows : rows + WIDTH], jnp.zeros((), bf16)
        )
        vt_ref[WIDTH:, lanes] = jnp.where(mask, jnp.ones((), bf16), jnp.zeros((), bf16))
        count = count + mask1.astype(f32)
    return count


def add_keys(keys, tiles, qt_ref, bias_ref, k_ref, vt_ref, acc_in, put):
    def tile(i, _):
        cols = pl.ds(pl.multiple_of(i * COLS, COLS), COLS)
        qt, bias = qt_ref[:, cols], bias_ref[1:2, cols]
        weights = jnp.exp2(dot(k_ref[:keys], qt) * SCALE - bias).astype(bf16)
        put(i, acc_in[:, cols] + dot(vt_ref[:, :keys], weights))
        return 0

    lax.fori_loop(0, tiles, tile, 0)


def parity_places(core, base):
    mine = pl.multiple_of(base + (1 - core) * BLOCK, BLOCK)
    other = pl.multiple_of(base + core * BLOCK, BLOCK)
    return mine, other


def first_and_reach(docs_ref):
    docs = docs_ref[...]
    doc = docs[:, :1]
    rows = jnp.sum((docs == doc).astype(f32)).astype(jnp.int32)
    return doc.astype(bf16), (rows + TILE - 1) // TILE


def steps_needed(count, step):
    keys = jnp.sum(count).astype(jnp.int32)
    return (keys + step - 1) // step


def add_gathered(count, most, step, tiles, qt_ref, bias_ref, k_ref, vt_ref, acc_in, put):
    need = steps_needed(count, step)
    for steps in range(1, most * BLOCK // step + 1):

        @pl.when(need == steps)
        def _(steps=steps):
            add_keys(steps * step, tiles, qt_ref, bias_ref, k_ref, vt_ref, acc_in, put)

    def tile(i, _):
        put(i, acc_in[:, pl.ds(pl.multiple_of(i * COLS, COLS), COLS)])
        return 0

    lax.fori_loop(jnp.where(need > 0, tiles, 0), TILES, tile, 0)


def putter(acc_out):
    def put(i, acc):
        acc_out[:, pl.ds(pl.multiple_of(i * COLS, COLS), COLS)] = acc

    return put


def gather_chips(core, doc, base, mine, theirs, first, k_ref, vt_ref):
    count = jnp.zeros((1, TILE), f32)
    for j in range(first, mine.shape[0]):
        x, y = parity_places(core, base)
        count += gather_block(mine.at[j], x, doc, k_ref, vt_ref)
        count += gather_block(theirs.at[j], y, doc, k_ref, vt_ref)
        base = base + 2 * BLOCK
    return count


def gather_near(core, doc, mine, theirs, k_ref, vt_ref):
    count = gather_block(theirs.at[0], 0, jnp.where(core == 1, doc, -jnp.ones_like(doc)), k_ref, vt_ref)
    return count + gather_chips(core, doc, core * BLOCK, mine, theirs, 1, k_ref, vt_ref)


def near_part(core_ref, docs_ref, qt_ref, bias_ref, acc_in, mine, theirs, acc_out, k_ref, vt_ref):
    doc, tiles = first_and_reach(docs_ref)
    count = gather_near(core_ref[0], doc, mine, theirs, k_ref, vt_ref)
    add_gathered(count, 3, 256, tiles, qt_ref, bias_ref, k_ref, vt_ref, acc_in, putter(acc_out))


def next_part(core_ref, docs_ref, qt_ref, bias_ref, acc_in, mine, theirs, acc_out, k_ref, vt_ref):
    doc, tiles = first_and_reach(docs_ref)
    count = gather_chips(core_ref[0], doc, 0, mine, theirs, 0, k_ref, vt_ref)
    add_gathered(count, 2, 256, tiles, qt_ref, bias_ref, k_ref, vt_ref, acc_in, putter(acc_out))


def last_part(
    core_ref, docs_ref, start_ref, qt_ref, bias_ref, acc_in, own_ref, mine0, theirs0, mine1, theirs1, mine2, theirs2,
    out_ref, k_ref, vt_ref, acc_ref, flag_ref, done_ref, fine_ref, sems,
):
    core = core_ref[0]
    doc, tiles = first_and_reach(docs_ref)
    count = gather_chips(core, doc, 0, mine2, theirs2, 0, k_ref, vt_ref)
    fine_ref[0] = jnp.int32(1)

    def write(i):
        rows = pl.ds(pl.multiple_of(i * TILE, TILE), TILE)
        return pltpu.make_async_copy(done_ref.at[rows], out_ref.at[rows], sems.at[i])

    def finish(i, acc):
        total = acc[WIDTH : WIDTH + 1]
        good = jnp.min((total < LIMIT).astype(jnp.int32))
        fine_ref[0] = jnp.minimum(fine_ref[0], good)
        final = (acc[:WIDTH] * (1.0 / total)).astype(bf16)
        rows = pl.ds(pl.multiple_of(i * TILE, TILE), TILE)
        for h in range(HEADS):
            done_ref[rows, h * WIDTH : (h + 1) * WIDTH] = final[:, h * TILE : (h + 1) * TILE].T
        write(i).start()

    add_gathered(count, 4, 256, tiles, qt_ref, bias_ref, k_ref, vt_ref, acc_in, finish)
    for i in range(TILES):
        write(i).wait()

    @pl.when(fine_ref[0] == 0)
    def _():
        pair_doc = jnp.where(core == 1, doc, -jnp.ones_like(doc))
        blocks = [(theirs0.at[0], pair_doc)]
        for mine, theirs, first in ((mine0, theirs0, 1), (mine1, theirs1, 0), (mine2, theirs2, 0)):
            for j in range(first, mine.shape[0]):
                blocks += [(mine.at[j], doc), (theirs.at[j], doc)]
        for i in range(TILES):
            cols = slice(i * COLS, (i + 1) * COLS)
            flag_ref[0:1, cols] = bias_ref[0:1, cols]
        first = first_acc(own_ref, start_ref, qt_ref, bias_ref, vt_ref)
        for i in range(TILES):
            acc_ref[:, i * COLS : (i + 1) * COLS] = first(i)
        for block_ref, block_doc in blocks:
            gather_block(block_ref, 0, block_doc, k_ref, vt_ref)
            mask = vt_ref[WIDTH : WIDTH + 1, :BLOCK].astype(f32)
            mask = jnp.concatenate(
                [jnp.broadcast_to(mask[:, c * TILE : (c + 1) * TILE], (TILE, TILE)).T for c in range(4)], axis=0
            )

            def tile(i, _, mask=mask):
                cols = pl.ds(pl.multiple_of(i * COLS, COLS), COLS)
                joins = bias_ref[1:2, cols] < 1e29
                allowed = (jnp.concatenate([mask] * HEADS, axis=1) > 0.5) & joins
                scores = jnp.where(allowed, dot(k_ref[:BLOCK], qt_ref[:, cols]), NEVER)
                old = flag_ref[0:1, cols]
                new = jnp.maximum(old, jnp.max(scores, axis=0, keepdims=True) * SCALE)
                weights = jnp.exp2(scores * SCALE - new).astype(bf16)
                acc_ref[:, cols] = acc_ref[:, cols] * jnp.exp2(old - new) + dot(vt_ref[:, :BLOCK], weights)
                flag_ref[0:1, cols] = new
                return 0

            lax.fori_loop(0, TILES, tile, 0)

        def last_tile(i, _):
            finish(i, acc_ref[:, pl.ds(pl.multiple_of(i * COLS, COLS), COLS)])
            write(i).wait()
            return 0

        lax.fori_loop(0, TILES, last_tile, 0)


def first_acc(own_ref, start_ref, qt_ref, bias_ref, vt_ref):
    for c in range(4):
        at = BLOCK + c * AUG
        vt_ref[:WIDTH, c * TILE : (c + 1) * TILE] = own_ref[at : at + WIDTH]
        vt_ref[WIDTH:, c * TILE : (c + 1) * TILE] = jnp.ones((16, TILE), bf16)

    def tile(i):
        cols = slice(i * COLS, (i + 1) * COLS)
        count = (i + 1) * TILE
        scores = dot(own_ref[:count], qt_ref[:, cols]) * SCALE + own_mask(start_ref, i)
        weights = jnp.exp2(scores - bias_ref[0:1, cols]).astype(bf16)
        return dot(vt_ref[:, :count], weights)

    return tile


def back(value, steps):
    count = lax.axis_size("cp")
    return lax.ppermute(value, "cp", [(s, s + steps) for s in range(count - steps)])


def other_core(value):
    return lax.ppermute(value, "cp", [(s, s ^ 1) for s in range(lax.axis_size("cp"))])


def per_device(queries, keys, values, doc_ids):
    shape = jax.ShapeDtypeStruct
    core = (lax.axis_index("cp") % 2).astype(jnp.int32).reshape(1)
    docs = (doc_ids + 1).astype(f32).reshape(1, BLOCK)
    start = jnp.sum(doc_ids[None, :] < doc_ids[:, None], axis=1).astype(jnp.int32).reshape(1, BLOCK)

    split = call(
        split_heads,
        shape((TP, 2 * CHUNK, WIDTH), bf16),
        (keys, values),
        [pltpu.VMEM((2, CHUNK, TP * WIDTH), bf16), pltpu.SemaphoreType.DMA((2,))],
        vmem=SPLIT_VMEM,
        specs=[HBM, HBM],
    )
    qt = call(
        transpose_queries,
        shape((WIDTH, ALL), bf16),
        (queries,),
        [pltpu.VMEM((BLOCK, HEADS * WIDTH), bf16), pltpu.SemaphoreType.DMA],
        specs=[HBM],
    )
    mine = lax.all_to_all(split, "tp", split_axis=0, concat_axis=0, tiled=True)
    packed = shape((PACK, WIDTH), bf16)
    own = call(pack_block, packed, (mine, docs, qt, start), specs=[VMEM, VMEM, ANY, ANY])

    def gathered(*blocks, after=()):
        count = len(blocks)
        outs = shape((count, PACK, WIDTH), bf16)
        specs = [VMEM] * count + [ANY] * len(after)
        mine = call(functools.partial(stack, count), outs, (*blocks, *after), specs=specs)
        return mine, other_core(mine)

    def scratch(blocks):
        return [pltpu.VMEM((blocks * BLOCK, WIDTH), bf16), pltpu.VMEM((AUG, blocks * BLOCK), bf16)]

    a4, a2 = back(own, 4), back(own, 2)
    a8, a6 = back(a4, 4), back(a4, 2)
    state = (shape((8, ALL), f32), shape((AUG, ALL), f32))
    operands = (qt, own, docs, start)
    bias, acc = call(own_part, state, operands, [pltpu.VMEM((AUG, BLOCK), bf16)], cost=OWN_COST)

    def add(part, acc, keys, blocks, cost):
        operands = (core, docs, qt, bias, acc, *keys)
        specs = [SMEM] + [VMEM] * 6
        return call(part, state[1], operands, scratch(blocks), cost=cost, specs=specs)

    near = gathered(own, a4, after=(bias,) if NEAR_AFTER else ())
    acc1 = add(near_part, acc, near, 4, NEAR_COST)
    mid = gathered(a2)
    acc = add(next_part, acc1, mid, 2, NEXT_COST)
    far = gathered(a6, a8, after=((acc1,), (acc,))[FAR_AFTER])
    return call(
        last_part,
        shape((BLOCK, HEADS * WIDTH), bf16),
        (core, docs, start, qt, bias, acc, own, *near, *mid, *far),
        [
            *scratch(4),
            pltpu.VMEM((AUG, ALL), f32),
            pltpu.VMEM((8, ALL), f32),
            pltpu.VMEM((BLOCK, HEADS * WIDTH), bf16),
            pltpu.SMEM((1,), jnp.int32),
            pltpu.SemaphoreType.DMA((TILES,)),
        ],
        cost=NEXT_COST,
        specs=[SMEM] + [VMEM] * 12,
        out_specs=HBM,
    )


def solution(mesh):
    placed = (P("cp", "tp"), P(("cp", "tp"), None), P(("cp", "tp"), None), P("cp"))
    return jax.shard_map(per_device, mesh=mesh, in_specs=placed, out_specs=P("cp", "tp"), check_vma=False)
```

```python
import functools

import jax
import jax.numpy as jnp
from jax import lax
from jax.experimental import pallas as pl
from jax.experimental.pallas import tpu as pltpu
from jax.sharding import PartitionSpec as P

HEADS = 8
TP = 8
WIDTH = 128
BLOCK = 512
CHUNK = BLOCK // TP
TILE = 128
TILES = BLOCK // TILE
COLS = HEADS * TILE
ALL = TILES * COLS
AUG = WIDTH + 16
DOCS = BLOCK + 4 * WIDTH
PACK = DOCS + 16
SCALE = WIDTH**-0.5 * 1.4426950408889634
NEVER = -1e30
LIMIT = 2.0**100
f32, bf16 = jnp.float32, jnp.bfloat16
SPLIT_VMEM = 60
OWN_COST = (10**11, 1 << 20)
NEAR_COST = (10**4, 10**4)
NEXT_COST = (10**4, 10**4)
FAR_AFTER = 0
NEAR_AFTER = 0
VMEM = pl.BlockSpec(memory_space=pltpu.VMEM)
SMEM = pl.BlockSpec(memory_space=pltpu.SMEM)
ANY = pl.BlockSpec(memory_space=pl.ANY)
HBM = pl.BlockSpec(memory_space=pltpu.HBM)


def dot(a, b):
    return jnp.dot(a, b, preferred_element_type=f32)


def call(kernel, outs, operands, scratch=(), cost=(10**4, 10**4), vmem=32, specs=None, out_specs=None):
    return pl.pallas_call(
        kernel,
        out_shape=outs,
        in_specs=specs or [VMEM] * len(operands),
        out_specs=out_specs or jax.tree.map(lambda _: VMEM, outs),
        scratch_shapes=list(scratch),
        compiler_params=pltpu.CompilerParams(vmem_limit_bytes=vmem << 20),
        cost_estimate=pl.CostEstimate(flops=cost[0], bytes_accessed=cost[1], transcendentals=0),
    )(*operands)


def split_heads(k_hbm, v_hbm, out_ref, kv_ref, sems):
    copies = [pltpu.make_async_copy(ref, kv_ref.at[j], sems.at[j]) for j, ref in enumerate((k_hbm, v_hbm))]
    for copy in copies:
        copy.start()
    for copy in copies:
        copy.wait()
    for h in range(TP):
        for j in range(2):
            out_ref[h, j * CHUNK : (j + 1) * CHUNK] = kv_ref[j, :, h * WIDTH : (h + 1) * WIDTH]


def transpose_queries(q_hbm, qt_ref, q_ref, sem):
    copy = pltpu.make_async_copy(q_hbm, q_ref, sem)
    copy.start()
    copy.wait()
    for i in range(TILES):
        for h in range(HEADS):
            at = i * COLS + h * TILE
            qt_ref[:, at : at + TILE] = q_ref[i * TILE : (i + 1) * TILE, h * WIDTH : (h + 1) * WIDTH].T


def stack(count, *refs):
    out_ref = refs[-1]
    for j, block in enumerate(refs[:count]):
        out_ref[j] = block[...]


def pack_block(kv_ref, docs_ref, dep0_ref, dep1_ref, out_ref):
    del dep0_ref, dep1_ref
    for t in range(TP):
        out_ref[t * CHUNK : (t + 1) * CHUNK] = kv_ref[t, :CHUNK]
    for c in range(4):
        at = BLOCK + c * WIDTH
        v = jnp.concatenate([kv_ref[2 * c, CHUNK:], kv_ref[2 * c + 1, CHUNK:]], axis=0)
        out_ref[at : at + WIDTH] = v.T
    rows = [docs_ref[:, c * TILE : (c + 1) * TILE] for c in range(4)]
    out_ref[DOCS:] = jnp.concatenate([*rows, jnp.zeros((12, TILE), f32)], axis=0).astype(bf16)


def tiled(row):
    return jnp.concatenate([row] * HEADS, axis=1)


def own_mask(start_ref, i):
    count = (i + 1) * TILE
    u = lax.broadcasted_iota(jnp.int32, (count, TILE), 0)
    t = lax.broadcasted_iota(jnp.int32, (count, TILE), 1) + i * TILE
    allowed = (u <= t) & (u >= start_ref[:, i * TILE : (i + 1) * TILE])
    return jnp.concatenate([jnp.where(allowed, 0.0, NEVER)] * HEADS, axis=1)


def own_part(qt_ref, own_ref, docs_ref, start_ref, bias_ref, acc_ref, vt_ref):
    ones = jnp.ones((16, TILE), bf16)
    for c in range(4):
        at = BLOCK + c * WIDTH
        vt_ref[:WIDTH, c * TILE : (c + 1) * TILE] = own_ref[at : at + WIDTH]
        vt_ref[WIDTH:, c * TILE : (c + 1) * TILE] = ones
    first_doc = docs_ref[:, :1]
    for i in range(TILES):
        here = slice(i * TILE, (i + 1) * TILE)
        cols = slice(i * COLS, (i + 1) * COLS)
        count = (i + 1) * TILE
        scores = dot(own_ref[:count], qt_ref[:, cols]) * SCALE + own_mask(start_ref, i)
        bias = jnp.max(scores, axis=0, keepdims=True)
        weights = jnp.exp2(scores - bias).astype(bf16)
        acc_ref[:, cols] = dot(vt_ref[:, :count], weights)
        joins = tiled(jnp.broadcast_to(first_doc, (1, TILE)) == docs_ref[:, here])
        bias_ref[0:1, cols] = bias
        bias_ref[1:2, cols] = jnp.where(joins, bias, -NEVER)
        bias_ref[2:8, cols] = jnp.zeros((6, COLS), f32)


def gather_block(block_ref, at, doc, k_ref, vt_ref):
    count = jnp.zeros((1, TILE), f32)
    docs = block_ref[DOCS:].astype(f32)
    for c in range(4):
        at_v = BLOCK + c * WIDTH
        mask = jnp.where(docs[c : c + 1] == doc, 1.0, 0.0)
        mask16 = jnp.broadcast_to(mask, (16, TILE)).astype(bf16)
        lanes = pl.ds(at + (3 - c) * TILE, TILE)
        k_ref[lanes, :] = block_ref[c * TILE : (c + 1) * TILE]
        vt_ref[:WIDTH, lanes] = block_ref[at_v : at_v + WIDTH] * jnp.concatenate([mask16] * 8, axis=0)
        vt_ref[WIDTH:, lanes] = mask16
        count = count + mask
    return count


def add_keys(keys, tiles, qt_ref, bias_ref, k_ref, vt_ref, acc_in, put):
    def tile(i, _):
        cols = pl.ds(pl.multiple_of(i * COLS, COLS), COLS)
        qt, bias = qt_ref[:, cols], bias_ref[1:2, cols]
        weights = jnp.exp2(dot(k_ref[:keys], qt) * SCALE - bias).astype(bf16)
        put(i, acc_in[:, cols] + dot(vt_ref[:, :keys], weights))
        return 0

    lax.fori_loop(0, tiles, tile, 0)


def parity_places(core, base):
    mine = pl.multiple_of(base + (1 - core) * BLOCK, BLOCK)
    other = pl.multiple_of(base + core * BLOCK, BLOCK)
    return mine, other


def first_and_reach(docs_ref):
    docs = docs_ref[...]
    doc = docs[:, :1]
    rows = jnp.sum((docs == doc).astype(f32)).astype(jnp.int32)
    return doc, (rows + TILE - 1) // TILE


def steps_needed(count, step):
    keys = jnp.sum(count).astype(jnp.int32)
    return (keys + step - 1) // step


def add_gathered(count, most, step, tiles, qt_ref, bias_ref, k_ref, vt_ref, acc_in, put):
    need = steps_needed(count, step)
    for steps in range(1, most * BLOCK // step + 1):

        @pl.when(need == steps)
        def _(steps=steps):
            add_keys(steps * step, tiles, qt_ref, bias_ref, k_ref, vt_ref, acc_in, put)

    def tile(i, _):
        put(i, acc_in[:, pl.ds(pl.multiple_of(i * COLS, COLS), COLS)])
        return 0

    lax.fori_loop(jnp.where(need > 0, tiles, 0), TILES, tile, 0)


def putter(acc_out):
    def put(i, acc):
        acc_out[:, pl.ds(pl.multiple_of(i * COLS, COLS), COLS)] = acc

    return put


def gather_chips(core, doc, base, mine, theirs, first, k_ref, vt_ref):
    count = jnp.zeros((1, TILE), f32)
    for j in range(first, mine.shape[0]):
        x, y = parity_places(core, base)
        count += gather_block(mine.at[j], x, doc, k_ref, vt_ref)
        count += gather_block(theirs.at[j], y, doc, k_ref, vt_ref)
        base = base + 2 * BLOCK
    return count


def gather_near(core, doc, mine, theirs, k_ref, vt_ref):
    count = gather_block(theirs.at[0], 0, jnp.where(core == 1, doc, -jnp.ones_like(doc)), k_ref, vt_ref)
    return count + gather_chips(core, doc, core * BLOCK, mine, theirs, 1, k_ref, vt_ref)


def near_part(core_ref, docs_ref, qt_ref, bias_ref, acc_in, mine, theirs, acc_out, k_ref, vt_ref):
    doc, tiles = first_and_reach(docs_ref)
    count = gather_near(core_ref[0], doc, mine, theirs, k_ref, vt_ref)
    add_gathered(count, 3, 256, tiles, qt_ref, bias_ref, k_ref, vt_ref, acc_in, putter(acc_out))


def next_part(core_ref, docs_ref, qt_ref, bias_ref, acc_in, mine, theirs, acc_out, k_ref, vt_ref):
    doc, tiles = first_and_reach(docs_ref)
    x, y = parity_places(core_ref[0], 0)
    count = gather_block(mine, x, doc, k_ref, vt_ref) + gather_block(theirs, y, doc, k_ref, vt_ref)
    add_gathered(count, 2, 256, tiles, qt_ref, bias_ref, k_ref, vt_ref, acc_in, putter(acc_out))


def last_part(
    core_ref, docs_ref, start_ref, qt_ref, bias_ref, acc_in, own_ref, mine0, theirs0, mine1, theirs1, mine2, theirs2,
    out_ref, k_ref, vt_ref, acc_ref, flag_ref, done_ref, sems,
):
    core = core_ref[0]
    doc, tiles = first_and_reach(docs_ref)
    count = gather_chips(core, doc, 0, mine2, theirs2, 0, k_ref, vt_ref)

    def write(i):
        rows = pl.ds(pl.multiple_of(i * TILE, TILE), TILE)
        return pltpu.make_async_copy(done_ref.at[rows], out_ref.at[rows], sems.at[i])

    def finish(i, acc):
        total = acc[WIDTH : WIDTH + 1]
        flag_ref[1:2, pl.ds(pl.multiple_of(i * COLS, COLS), COLS)] = total
        final = (acc[:WIDTH] * (1.0 / total)).astype(bf16)
        rows = pl.ds(pl.multiple_of(i * TILE, TILE), TILE)
        for h in range(HEADS):
            done_ref[rows, h * WIDTH : (h + 1) * WIDTH] = final[:, h * TILE : (h + 1) * TILE].T
        write(i).start()

    add_gathered(count, 4, 256, tiles, qt_ref, bias_ref, k_ref, vt_ref, acc_in, finish)
    fine = jnp.min((flag_ref[1:2, :] < LIMIT).astype(f32))
    for i in range(TILES):
        write(i).wait()

    @pl.when(fine < 0.5)
    def _():
        pair_doc = jnp.where(core == 1, doc, -jnp.ones_like(doc))
        blocks = [(theirs0.at[0], pair_doc)]
        blocks += [(mine1, doc), (theirs1, doc)]
        for mine, theirs, first in ((mine0, theirs0, 1), (mine2, theirs2, 0)):
            for j in range(first, mine.shape[0]):
                blocks += [(mine.at[j], doc), (theirs.at[j], doc)]
        for i in range(TILES):
            cols = slice(i * COLS, (i + 1) * COLS)
            flag_ref[0:1, cols] = bias_ref[0:1, cols]
        first = first_acc(own_ref, start_ref, qt_ref, bias_ref, vt_ref)
        for i in range(TILES):
            acc_ref[:, i * COLS : (i + 1) * COLS] = first(i)
        for block_ref, block_doc in blocks:
            gather_block(block_ref, 0, block_doc, k_ref, vt_ref)
            mask = vt_ref[WIDTH : WIDTH + 1, :BLOCK].astype(f32)
            mask = jnp.concatenate(
                [jnp.broadcast_to(mask[:, c * TILE : (c + 1) * TILE], (TILE, TILE)).T for c in range(4)], axis=0
            )

            def tile(i, _, mask=mask):
                cols = pl.ds(pl.multiple_of(i * COLS, COLS), COLS)
                joins = bias_ref[1:2, cols] < 1e29
                allowed = (jnp.concatenate([mask] * HEADS, axis=1) > 0.5) & joins
                scores = jnp.where(allowed, dot(k_ref[:BLOCK], qt_ref[:, cols]), NEVER)
                old = flag_ref[0:1, cols]
                new = jnp.maximum(old, jnp.max(scores, axis=0, keepdims=True) * SCALE)
                weights = jnp.exp2(scores * SCALE - new).astype(bf16)
                acc_ref[:, cols] = acc_ref[:, cols] * jnp.exp2(old - new) + dot(vt_ref[:, :BLOCK], weights)
                flag_ref[0:1, cols] = new
                return 0

            lax.fori_loop(0, TILES, tile, 0)

        def last_tile(i, _):
            finish(i, acc_ref[:, pl.ds(pl.multiple_of(i * COLS, COLS), COLS)])
            write(i).wait()
            return 0

        lax.fori_loop(0, TILES, last_tile, 0)


def first_acc(own_ref, start_ref, qt_ref, bias_ref, vt_ref):
    for c in range(4):
        at = BLOCK + c * WIDTH
        vt_ref[:WIDTH, c * TILE : (c + 1) * TILE] = own_ref[at : at + WIDTH]
        vt_ref[WIDTH:, c * TILE : (c + 1) * TILE] = jnp.ones((16, TILE), bf16)

    def tile(i):
        cols = slice(i * COLS, (i + 1) * COLS)
        count = (i + 1) * TILE
        scores = dot(own_ref[:count], qt_ref[:, cols]) * SCALE + own_mask(start_ref, i)
        weights = jnp.exp2(scores - bias_ref[0:1, cols]).astype(bf16)
        return dot(vt_ref[:, :count], weights)

    return tile


def back(value, steps):
    count = lax.axis_size("cp")
    return lax.ppermute(value, "cp", [(s, s + steps) for s in range(count - steps)])


def other_core(value):
    return lax.ppermute(value, "cp", [(s, s ^ 1) for s in range(lax.axis_size("cp"))])


def per_device(queries, keys, values, doc_ids):
    shape = jax.ShapeDtypeStruct
    core = (lax.axis_index("cp") % 2).astype(jnp.int32).reshape(1)
    docs = (doc_ids + 1).astype(f32).reshape(1, BLOCK)
    start = jnp.sum(doc_ids[None, :] < doc_ids[:, None], axis=1).astype(jnp.int32).reshape(1, BLOCK)

    split = call(
        split_heads,
        shape((TP, 2 * CHUNK, WIDTH), bf16),
        (keys, values),
        [pltpu.VMEM((2, CHUNK, TP * WIDTH), bf16), pltpu.SemaphoreType.DMA((2,))],
        vmem=SPLIT_VMEM,
        specs=[HBM, HBM],
    )
    qt = call(
        transpose_queries,
        shape((WIDTH, ALL), bf16),
        (queries,),
        [pltpu.VMEM((BLOCK, HEADS * WIDTH), bf16), pltpu.SemaphoreType.DMA],
        specs=[HBM],
    )
    mine = lax.all_to_all(split, "tp", split_axis=0, concat_axis=0, tiled=True)
    packed = shape((PACK, WIDTH), bf16)
    own = call(pack_block, packed, (mine, docs, qt, start), specs=[VMEM, VMEM, ANY, ANY])

    def gathered(*blocks, after=()):
        count = len(blocks)
        outs = shape((count, PACK, WIDTH), bf16)
        specs = [VMEM] * count + [ANY] * len(after)
        mine = call(functools.partial(stack, count), outs, (*blocks, *after), specs=specs)
        return mine, other_core(mine)

    def scratch(blocks):
        return [pltpu.VMEM((blocks * BLOCK, WIDTH), bf16), pltpu.VMEM((AUG, blocks * BLOCK), bf16)]

    a4, a2 = back(own, 4), back(own, 2)
    a8, a6 = back(a4, 4), back(a4, 2)
    state = (shape((8, ALL), f32), shape((AUG, ALL), f32))
    operands = (qt, own, docs, start)
    bias, acc = call(own_part, state, operands, [pltpu.VMEM((AUG, BLOCK), bf16)], cost=OWN_COST)

    def add(part, acc, keys, blocks, cost):
        operands = (core, docs, qt, bias, acc, *keys)
        specs = [SMEM] + [VMEM] * 6
        return call(part, state[1], operands, scratch(blocks), cost=cost, specs=specs)

    near = gathered(own, a4, after=(bias,) if NEAR_AFTER else ())
    acc1 = add(near_part, acc, near, 4, NEAR_COST)
    mid = (a2, other_core(a2))
    acc = add(next_part, acc1, mid, 2, NEXT_COST)
    far = gathered(a6, a8, after=((acc1,), (acc,))[FAR_AFTER])
    return call(
        last_part,
        shape((BLOCK, HEADS * WIDTH), bf16),
        (core, docs, start, qt, bias, acc, own, *near, *mid, *far),
        [
            *scratch(4),
            pltpu.VMEM((AUG, ALL), f32),
            pltpu.VMEM((8, ALL), f32),
            pltpu.VMEM((BLOCK, HEADS * WIDTH), bf16),
            pltpu.SemaphoreType.DMA((TILES,)),
        ],
        cost=NEXT_COST,
        specs=[SMEM] + [VMEM] * 12,
        out_specs=HBM,
    )


def solution(mesh):
    placed = (P("cp", "tp"), P(("cp", "tp"), None), P(("cp", "tp"), None), P("cp"))
    return jax.shard_map(per_device, mesh=mesh, in_specs=placed, out_specs=P("cp", "tp"), check_vma=False)
```

```python
import functools

import jax
import jax.numpy as jnp
from jax import lax
from jax.experimental import pallas as pl
from jax.experimental.pallas import tpu as pltpu
from jax.sharding import PartitionSpec as P

HEADS = 8
TP = 8
WIDTH = 128
BLOCK = 512
CHUNK = BLOCK // TP
TILE = 128
TILES = BLOCK // TILE
COLS = HEADS * TILE
ALL = TILES * COLS
AUG = WIDTH + 16
DOCS = BLOCK + 4 * WIDTH
PACK = DOCS + 16
SCALE = WIDTH**-0.5 * 1.4426950408889634
NEVER = -1e30
LIMIT = 2.0**100
f32, bf16 = jnp.float32, jnp.bfloat16
SPLIT_VMEM = 60
OWN_COST = (10**11, 1 << 20)
NEAR_COST = (10**4, 10**4)
NEXT_COST = (10**4, 10**4)
FAR_AFTER = 0
NEAR_AFTER = 0
VMEM = pl.BlockSpec(memory_space=pltpu.VMEM)
SMEM = pl.BlockSpec(memory_space=pltpu.SMEM)
ANY = pl.BlockSpec(memory_space=pl.ANY)
HBM = pl.BlockSpec(memory_space=pltpu.HBM)


def dot(a, b):
    return jnp.dot(a, b, preferred_element_type=f32)


def call(kernel, outs, operands, scratch=(), cost=(10**4, 10**4), vmem=32, specs=None, out_specs=None):
    return pl.pallas_call(
        kernel,
        out_shape=outs,
        in_specs=specs or [VMEM] * len(operands),
        out_specs=out_specs or jax.tree.map(lambda _: VMEM, outs),
        scratch_shapes=list(scratch),
        compiler_params=pltpu.CompilerParams(vmem_limit_bytes=vmem << 20),
        cost_estimate=pl.CostEstimate(flops=cost[0], bytes_accessed=cost[1], transcendentals=0),
    )(*operands)


def split_heads(k_hbm, v_hbm, out_ref, kv_ref, sems):
    copies = [pltpu.make_async_copy(ref, kv_ref.at[j], sems.at[j]) for j, ref in enumerate((k_hbm, v_hbm))]
    for copy in copies:
        copy.start()
    for copy in copies:
        copy.wait()
    for h in range(TP):
        for j in range(2):
            out_ref[h, j * CHUNK : (j + 1) * CHUNK] = kv_ref[j, :, h * WIDTH : (h + 1) * WIDTH]


def transpose_queries(q_hbm, qt_ref, q_ref, sem):
    copy = pltpu.make_async_copy(q_hbm, q_ref, sem)
    copy.start()
    copy.wait()
    for i in range(TILES):
        for h in range(HEADS):
            at = i * COLS + h * TILE
            qt_ref[:, at : at + TILE] = q_ref[i * TILE : (i + 1) * TILE, h * WIDTH : (h + 1) * WIDTH].T


def stack(count, *refs):
    out_ref = refs[-1]
    for j, block in enumerate(refs[:count]):
        out_ref[j] = block[...]


def pack_block(kv_ref, docs_ref, dep0_ref, dep1_ref, out_ref):
    del dep0_ref, dep1_ref
    for t in range(TP):
        out_ref[t * CHUNK : (t + 1) * CHUNK] = kv_ref[t, :CHUNK]
    for c in range(4):
        at = BLOCK + c * WIDTH
        v = jnp.concatenate([kv_ref[2 * c, CHUNK:], kv_ref[2 * c + 1, CHUNK:]], axis=0)
        out_ref[at : at + WIDTH] = v.T
    rows = [docs_ref[:, c * TILE : (c + 1) * TILE] for c in range(4)]
    out_ref[DOCS:] = jnp.concatenate([*rows, jnp.zeros((12, TILE), f32)], axis=0).astype(bf16)


def tiled(row):
    return jnp.concatenate([row] * HEADS, axis=1)


def own_mask(start_ref, i):
    count = (i + 1) * TILE
    u = lax.broadcasted_iota(jnp.int32, (count, TILE), 0)
    t = lax.broadcasted_iota(jnp.int32, (count, TILE), 1) + i * TILE
    allowed = (u <= t) & (u >= start_ref[:, i * TILE : (i + 1) * TILE])
    return jnp.concatenate([jnp.where(allowed, 0.0, NEVER)] * HEADS, axis=1)


def own_part(qt_ref, own_ref, docs_ref, start_ref, bias_ref, acc_ref, vt_ref):
    ones = jnp.ones((16, TILE), bf16)
    for c in range(4):
        at = BLOCK + c * WIDTH
        vt_ref[:WIDTH, c * TILE : (c + 1) * TILE] = own_ref[at : at + WIDTH]
        vt_ref[WIDTH:, c * TILE : (c + 1) * TILE] = ones
    first_doc = docs_ref[:, :1]
    for i in range(TILES):
        here = slice(i * TILE, (i + 1) * TILE)
        cols = slice(i * COLS, (i + 1) * COLS)
        count = (i + 1) * TILE
        scores = dot(own_ref[:count], qt_ref[:, cols]) * SCALE + own_mask(start_ref, i)
        bias = jnp.max(scores, axis=0, keepdims=True)
        weights = jnp.exp2(scores - bias).astype(bf16)
        acc_ref[:, cols] = dot(vt_ref[:, :count], weights)
        joins = tiled(jnp.broadcast_to(first_doc, (1, TILE)) == docs_ref[:, here])
        bias_ref[0:1, cols] = bias
        bias_ref[1:2, cols] = jnp.where(joins, bias, -NEVER)
        bias_ref[2:8, cols] = jnp.zeros((6, COLS), f32)


def gather_block(block_ref, at, doc, k_ref, vt_ref):
    count = jnp.zeros((1, TILE), f32)
    docs = block_ref[DOCS:].astype(f32)
    for c in range(4):
        at_v = BLOCK + c * WIDTH
        mask = jnp.where(docs[c : c + 1] == doc, 1.0, 0.0)
        mask16 = jnp.broadcast_to(mask, (16, TILE)).astype(bf16)
        lanes = pl.ds(at + (3 - c) * TILE, TILE)
        k_ref[lanes, :] = block_ref[c * TILE : (c + 1) * TILE]
        vt_ref[:WIDTH, lanes] = block_ref[at_v : at_v + WIDTH] * jnp.concatenate([mask16] * 8, axis=0)
        vt_ref[WIDTH:, lanes] = mask16
        count = count + mask
    return count


def add_keys(keys, tiles, qt_ref, bias_ref, k_ref, vt_ref, acc_in, put):
    def tile(i, _):
        cols = pl.ds(pl.multiple_of(i * COLS, COLS), COLS)
        qt, bias = qt_ref[:, cols], bias_ref[1:2, cols]
        weights = jnp.exp2(dot(k_ref[:keys], qt) * SCALE - bias).astype(bf16)
        put(i, acc_in[:, cols] + dot(vt_ref[:, :keys], weights))
        return 0

    lax.fori_loop(0, tiles, tile, 0)


def parity_places(core, base):
    mine = pl.multiple_of(base + (1 - core) * BLOCK, BLOCK)
    other = pl.multiple_of(base + core * BLOCK, BLOCK)
    return mine, other


def first_and_reach(docs_ref):
    docs = docs_ref[...]
    doc = docs[:, :1]
    rows = jnp.sum((docs == doc).astype(f32)).astype(jnp.int32)
    return doc, (rows + TILE - 1) // TILE


def steps_needed(count, step):
    keys = jnp.sum(count).astype(jnp.int32)
    return (keys + step - 1) // step


def add_gathered(count, most, step, tiles, qt_ref, bias_ref, k_ref, vt_ref, acc_in, put):
    need = steps_needed(count, step)
    for steps in range(1, most * BLOCK // step + 1):

        @pl.when(need == steps)
        def _(steps=steps):
            add_keys(steps * step, tiles, qt_ref, bias_ref, k_ref, vt_ref, acc_in, put)

    def tile(i, _):
        put(i, acc_in[:, pl.ds(pl.multiple_of(i * COLS, COLS), COLS)])
        return 0

    lax.fori_loop(jnp.where(need > 0, tiles, 0), TILES, tile, 0)


def putter(acc_out):
    def put(i, acc):
        acc_out[:, pl.ds(pl.multiple_of(i * COLS, COLS), COLS)] = acc

    return put


def gather_chips(core, doc, base, mine, theirs, order, k_ref, vt_ref):
    count = jnp.zeros((1, TILE), f32)
    for j in order:
        x, y = parity_places(core, base)
        count += gather_block(mine.at[j], x, doc, k_ref, vt_ref)
        count += gather_block(theirs.at[j], y, doc, k_ref, vt_ref)
        base = base + 2 * BLOCK
    return count


def gather_near(core, doc, mine, theirs, k_ref, vt_ref):
    count = gather_block(theirs.at[0], 0, jnp.where(core == 1, doc, -jnp.ones_like(doc)), k_ref, vt_ref)
    return count + gather_chips(core, doc, core * BLOCK, mine, theirs, (1,), k_ref, vt_ref)


def near_part(core_ref, docs_ref, qt_ref, bias_ref, acc_in, mine, theirs, acc_out, k_ref, vt_ref):
    doc, tiles = first_and_reach(docs_ref)
    count = gather_near(core_ref[0], doc, mine, theirs, k_ref, vt_ref)
    add_gathered(count, 3, 256, tiles, qt_ref, bias_ref, k_ref, vt_ref, acc_in, putter(acc_out))


def next_part(core_ref, docs_ref, qt_ref, bias_ref, acc_in, mine, theirs, acc_out, k_ref, vt_ref):
    doc, tiles = first_and_reach(docs_ref)
    x, y = parity_places(core_ref[0], 0)
    count = gather_block(mine, x, doc, k_ref, vt_ref) + gather_block(theirs, y, doc, k_ref, vt_ref)
    add_gathered(count, 2, 256, tiles, qt_ref, bias_ref, k_ref, vt_ref, acc_in, putter(acc_out))


def last_part(
    core_ref, docs_ref, start_ref, qt_ref, bias_ref, acc_in, own_ref, mine0, theirs0, mine1, theirs1, mine2, theirs2,
    out_ref, k_ref, vt_ref, acc_ref, flag_ref, done_ref, sems,
):
    core = core_ref[0]
    doc, tiles = first_and_reach(docs_ref)
    count = gather_chips(core, doc, 0, mine2, theirs2, (1, 0), k_ref, vt_ref)

    def write(i):
        rows = pl.ds(pl.multiple_of(i * TILE, TILE), TILE)
        return pltpu.make_async_copy(done_ref.at[rows], out_ref.at[rows], sems.at[i])

    def finish(i, acc):
        total = acc[WIDTH : WIDTH + 1]
        flag_ref[1:2, pl.ds(pl.multiple_of(i * COLS, COLS), COLS)] = total
        final = (acc[:WIDTH] * (1.0 / total)).astype(bf16)
        rows = pl.ds(pl.multiple_of(i * TILE, TILE), TILE)
        for h in range(HEADS):
            done_ref[rows, h * WIDTH : (h + 1) * WIDTH] = final[:, h * TILE : (h + 1) * TILE].T
        write(i).start()

    add_gathered(count, 4, 256, tiles, qt_ref, bias_ref, k_ref, vt_ref, acc_in, finish)
    fine = jnp.min((flag_ref[1:2, :] < LIMIT).astype(f32))
    for i in range(TILES):
        write(i).wait()

    @pl.when(fine < 0.5)
    def _():
        pair_doc = jnp.where(core == 1, doc, -jnp.ones_like(doc))
        blocks = [(theirs0.at[0], pair_doc)]
        blocks += [(mine1, doc), (theirs1, doc)]
        for mine, theirs, first in ((mine0, theirs0, 1), (mine2, theirs2, 0)):
            for j in range(first, mine.shape[0]):
                blocks += [(mine.at[j], doc), (theirs.at[j], doc)]
        for i in range(TILES):
            cols = slice(i * COLS, (i + 1) * COLS)
            flag_ref[0:1, cols] = bias_ref[0:1, cols]
        first = first_acc(own_ref, start_ref, qt_ref, bias_ref, vt_ref)
        for i in range(TILES):
            acc_ref[:, i * COLS : (i + 1) * COLS] = first(i)
        for block_ref, block_doc in blocks:
            gather_block(block_ref, 0, block_doc, k_ref, vt_ref)
            mask = vt_ref[WIDTH : WIDTH + 1, :BLOCK].astype(f32)
            mask = jnp.concatenate(
                [jnp.broadcast_to(mask[:, c * TILE : (c + 1) * TILE], (TILE, TILE)).T for c in range(4)], axis=0
            )

            def tile(i, _, mask=mask):
                cols = pl.ds(pl.multiple_of(i * COLS, COLS), COLS)
                joins = bias_ref[1:2, cols] < 1e29
                allowed = (jnp.concatenate([mask] * HEADS, axis=1) > 0.5) & joins
                scores = jnp.where(allowed, dot(k_ref[:BLOCK], qt_ref[:, cols]), NEVER)
                old = flag_ref[0:1, cols]
                new = jnp.maximum(old, jnp.max(scores, axis=0, keepdims=True) * SCALE)
                weights = jnp.exp2(scores * SCALE - new).astype(bf16)
                acc_ref[:, cols] = acc_ref[:, cols] * jnp.exp2(old - new) + dot(vt_ref[:, :BLOCK], weights)
                flag_ref[0:1, cols] = new
                return 0

            lax.fori_loop(0, TILES, tile, 0)

        def last_tile(i, _):
            finish(i, acc_ref[:, pl.ds(pl.multiple_of(i * COLS, COLS), COLS)])
            write(i).wait()
            return 0

        lax.fori_loop(0, TILES, last_tile, 0)


def first_acc(own_ref, start_ref, qt_ref, bias_ref, vt_ref):
    for c in range(4):
        at = BLOCK + c * WIDTH
        vt_ref[:WIDTH, c * TILE : (c + 1) * TILE] = own_ref[at : at + WIDTH]
        vt_ref[WIDTH:, c * TILE : (c + 1) * TILE] = jnp.ones((16, TILE), bf16)

    def tile(i):
        cols = slice(i * COLS, (i + 1) * COLS)
        count = (i + 1) * TILE
        scores = dot(own_ref[:count], qt_ref[:, cols]) * SCALE + own_mask(start_ref, i)
        weights = jnp.exp2(scores - bias_ref[0:1, cols]).astype(bf16)
        return dot(vt_ref[:, :count], weights)

    return tile


def back(value, steps):
    count = lax.axis_size("cp")
    return lax.ppermute(value, "cp", [(s, s + steps) for s in range(count - steps)])


def other_core(value):
    return lax.ppermute(value, "cp", [(s, s ^ 1) for s in range(lax.axis_size("cp"))])


def per_device(queries, keys, values, doc_ids):
    shape = jax.ShapeDtypeStruct
    core = (lax.axis_index("cp") % 2).astype(jnp.int32).reshape(1)
    docs = (doc_ids + 1).astype(f32).reshape(1, BLOCK)
    start = jnp.sum(doc_ids[None, :] < doc_ids[:, None], axis=1).astype(jnp.int32).reshape(1, BLOCK)

    split = call(
        split_heads,
        shape((TP, 2 * CHUNK, WIDTH), bf16),
        (keys, values),
        [pltpu.VMEM((2, CHUNK, TP * WIDTH), bf16), pltpu.SemaphoreType.DMA((2,))],
        vmem=SPLIT_VMEM,
        specs=[HBM, HBM],
    )
    qt = call(
        transpose_queries,
        shape((WIDTH, ALL), bf16),
        (queries,),
        [pltpu.VMEM((BLOCK, HEADS * WIDTH), bf16), pltpu.SemaphoreType.DMA],
        specs=[HBM],
    )
    mine = lax.all_to_all(split, "tp", split_axis=0, concat_axis=0, tiled=True)
    packed = shape((PACK, WIDTH), bf16)
    own = call(pack_block, packed, (mine, docs, qt, start), specs=[VMEM, VMEM, ANY, ANY])

    def gathered(*blocks, after=()):
        count = len(blocks)
        outs = shape((count, PACK, WIDTH), bf16)
        specs = [VMEM] * count + [ANY] * len(after)
        mine = call(functools.partial(stack, count), outs, (*blocks, *after), specs=specs)
        return mine, other_core(mine)

    def scratch(blocks):
        return [pltpu.VMEM((blocks * BLOCK, WIDTH), bf16), pltpu.VMEM((AUG, blocks * BLOCK), bf16)]

    a4, a2 = back(own, 4), back(own, 2)
    a6, a8 = back(a4, 2), back(a4, 4)
    state = (shape((8, ALL), f32), shape((AUG, ALL), f32))
    operands = (qt, own, docs, start)
    bias, acc = call(own_part, state, operands, [pltpu.VMEM((AUG, BLOCK), bf16)], cost=OWN_COST)

    def add(part, acc, keys, blocks, cost):
        operands = (core, docs, qt, bias, acc, *keys)
        specs = [SMEM] + [VMEM] * 6
        return call(part, state[1], operands, scratch(blocks), cost=cost, specs=specs)

    near = gathered(own, a4, after=(bias,) if NEAR_AFTER else ())
    acc1 = add(near_part, acc, near, 4, NEAR_COST)
    mid = (a2, other_core(a2))
    acc = add(next_part, acc1, mid, 2, NEXT_COST)
    far = gathered(a8, a6, after=((acc1,), (acc,))[FAR_AFTER])
    return call(
        last_part,
        shape((BLOCK, HEADS * WIDTH), bf16),
        (core, docs, start, qt, bias, acc, own, *near, *mid, *far),
        [
            *scratch(4),
            pltpu.VMEM((AUG, ALL), f32),
            pltpu.VMEM((8, ALL), f32),
            pltpu.VMEM((BLOCK, HEADS * WIDTH), bf16),
            pltpu.SemaphoreType.DMA((TILES,)),
        ],
        cost=NEXT_COST,
        specs=[SMEM] + [VMEM] * 12,
        out_specs=HBM,
    )


def solution(mesh):
    placed = (P("cp", "tp"), P(("cp", "tp"), None), P(("cp", "tp"), None), P("cp"))
    return jax.shard_map(per_device, mesh=mesh, in_specs=placed, out_specs=P("cp", "tp"), check_vma=False)
```
